32 devices in a mesh: parts: 1, ctx: 4 (over z), pb: 4 (over y, x), row: 2 (over core).
Axes of the slice: x: 2, y: 2, z: 4, core: 2. Of those that a mesh axis runs over, the one named last changes fastest.
Arguments:
- queries: bfloat16 [2048, 3072], P(('parts', 'ctx', 'pb', 'row')), may hold values from -10 to 10
- cache_keys: bfloat16 [4096, 192], P(('parts', 'ctx')), may hold values from -10 to 10
- cache_values: bfloat16 [4096, 128], P(('parts', 'ctx')), may hold values from -6 to 6
- span_keys: bfloat16 [2048, 192], P(('parts', 'ctx')), may hold values from -10 to 10
- span_values: bfloat16 [2048, 128], P(('parts', 'ctx')), may hold values from -6 to 6
- pool_keys: float32 [32, 192], replicated, may hold values from 0.2 to 0.6
- pool_values: float32 [32, 128], replicated, may hold values from 0.05 to 0.3
- gate_logits: bfloat16 [2048, 48], P(('parts', 'ctx', 'pb', 'row')), may hold values from -6 to 6
- chosen_blocks: int32 [32, 16], P(('parts', 'ctx', 'pb', 'row')), may hold values from 0 to 95, as said below
- valid_counts: int32 [32], P(('parts', 'ctx', 'pb', 'row')), may hold values from 4 to 16
Outputs:
- mixed: bfloat16 [2048, 2048], P(('parts', 'ctx', 'pb', 'row'))
The draws below stay inside these ranges and needn't reach their ends.
Inputs may be any that keep to these rules, and one draw needn't show every extreme that they name: `chosen_blocks`: slot 0 of tile t holds the tile's own block 64 + t. Slot s > 0 holds a block of the cache stored by ctx index (c + s) mod (4), where c is the ctx index that holds tile t; the blocks of one tile are distinct. Slots at or beyond the tile's valid count hold blocks too and are ignored.
All inputs are finite; a program needn't handle non-finite values.
Results may differ from the reference program's by a relative error of at most 0.0034.
The reference program's roundings to bfloat16 on the way (of `weights`) count: a program that leaves them out, or rounds other values in their place, can miss the bound.
Values may be sent and summed in bfloat16 or wider, within the bound.
A program may use at most 64 MiB of HBM per device.

```python
import math
import jax
import jax.numpy as jnp
from jax import lax

HEADS = 16
DK = 192
DV = 128
CLEN = 32
STRIDE = 16
BLOCK = 64
PICKS = 16
WINDOW = 256
CACHE_DEV = 1024
SPAN_DEV = 512
CACHE = 4096
SPAN = 2048
TILES = 32
NCB = 384
REACH = 4


def joint_keys(key):
    normal_rows = jnp.clip(jax.random.normal(jax.random.fold_in(key, 101), (CACHE + SPAN, DK), jnp.float32), -6.0, 6.0)
    return normal_rows


def draw_cache_keys(key, part):
    return joint_keys(key)[:CACHE].astype(jnp.bfloat16)


def draw_span_keys(key, part):
    return joint_keys(key)[CACHE:].astype(jnp.bfloat16)


def draw_queries(key, part):
    normal_rows = jnp.clip(2.0 * jax.random.normal(jax.random.fold_in(key, 201), (SPAN, HEADS, DK), jnp.float32), -8.0, 8.0)
    return normal_rows.reshape(SPAN, HEADS * DK).astype(jnp.bfloat16)


def draw_chosen_blocks(key, part):
    tile_count = SPAN // BLOCK
    owner_count = PICKS // REACH
    cache_count = CACHE_DEV // BLOCK
    tile_index = jnp.arange(tile_count, dtype=jnp.int32)[:, None]
    slot_index = jnp.arange(PICKS, dtype=jnp.int32)[None, :]
    home_ctx = tile_index * BLOCK // SPAN_DEV
    column = jnp.broadcast_to(slot_index % owner_count, (tile_count, PICKS))
    repeat_index = slot_index // owner_count
    owner_ctx = (home_ctx + column) % owner_count
    start_block = jax.random.randint(jax.random.fold_in(key, 301), (tile_count, owner_count), 0, cache_count, dtype=jnp.int32)
    chosen_start = jnp.take_along_axis(start_block, column, axis=1)
    picked = owner_ctx * cache_count + (chosen_start + repeat_index) % cache_count
    own_block = CACHE // BLOCK + tile_index
    return jnp.where(slot_index == 0, own_block, picked).astype(jnp.int32)


def set_ends(drawn, rng, low, top_value):
    spot = [jax.random.randint(jax.random.fold_in(rng, axis), (), 0, length) for axis, length in enumerate(drawn.shape)]
    longest = drawn.shape.index(max(drawn.shape))
    beside = spot[:longest] + [(spot[longest] + 1) % drawn.shape[longest]] + spot[longest + 1:]
    return drawn.at[tuple(spot)].set(low).at[tuple(beside)].set(top_value)


def levels(rng, dims, shards, low, high):
    gain = 1.0
    for axis_at, blocks in shards:
        steps = jax.random.uniform(jax.random.fold_in(jax.random.fold_in(rng, 6), axis_at), (blocks,), jnp.float32, low / len(shards), high / len(shards))
        gain = gain * jnp.repeat(jnp.exp(steps), dims[axis_at] // blocks).reshape((-1,) + (1,) * (len(dims) - 1 - axis_at))
    return gain


def bell_draw(rng, extent, deviation, limit, cuts=(), kind=jnp.bfloat16):
    drawn = deviation * jax.random.normal(rng, extent, jnp.float32)
    if cuts:
        drawn = drawn * levels(rng, extent, cuts, -0.22, 0.18)
    return jnp.clip(drawn, -limit, limit).astype(kind)


def setup_inputs(seed: int = 0, part: int = 0) -> dict:
    key_of = jax.random.split(jax.random.key(seed), 11)
    own_keys = jax.random.split(jax.random.fold_in(key_of[10], part), 11)
    queries = draw_queries(jax.random.fold_in(jax.random.fold_in(key_of[10], part), 71), part)
    cache_keys = draw_cache_keys(jax.random.fold_in(jax.random.fold_in(key_of[10], part), 71), part)
    cache_values = bell_draw(own_keys[2], (CACHE, DV), 1.0, 6.0, ((0, 4),))
    span_keys = draw_span_keys(jax.random.fold_in(jax.random.fold_in(key_of[10], part), 71), part)
    span_values = bell_draw(own_keys[4], (SPAN, DV), 1.0, 6.0, ((0, 4),))
    pool_keys = jnp.clip(jax.random.uniform(key_of[5], (CLEN, DK), jnp.float32, 0.2, 0.6), 0.2, 0.6)
    pool_values = jnp.clip(jax.random.uniform(key_of[6], (CLEN, DV), jnp.float32, 0.05, 0.3), 0.05, 0.3)
    gate_logits = bell_draw(own_keys[7], (SPAN, 3 * HEADS), 1.5, 6.0, ((0, 32),))
    chosen_blocks = draw_chosen_blocks(jax.random.fold_in(jax.random.fold_in(key_of[10], part), 71), part)
    valid_counts = set_ends(jax.random.randint(own_keys[9], (TILES,), 4, PICKS + 1), jax.random.fold_in(own_keys[9], 1), 4, PICKS).astype(jnp.int32)
    return dict(queries=queries, cache_keys=cache_keys, cache_values=cache_values, span_keys=span_keys, span_values=span_values, pool_keys=pool_keys, pool_values=pool_values, gate_logits=gate_logits, chosen_blocks=chosen_blocks, valid_counts=valid_counts)


NEG_FILL = -1e+30

def pool_blocks(rows, extra, weights, stride):
    joined = jnp.concatenate([rows, extra], axis=0).astype(jnp.float32)
    blocks = rows.shape[0] // stride
    grouped = joined.reshape(blocks + 1, stride, rows.shape[1])
    leading = lax.optimization_barrier(jnp.sum(grouped[:-1] * weights[None, :stride, :], axis=1))
    trailing = lax.optimization_barrier(jnp.sum(grouped[1:] * weights[None, stride:, :], axis=1))
    return (leading + trailing).astype(jnp.bfloat16)

def attend(query_rows, keys, values, visible, score_scale):
    scores = jnp.dot(query_rows, keys.T, preferred_element_type=jnp.float32) * score_scale
    scores = jnp.where(visible, scores, NEG_FILL)
    highest = lax.optimization_barrier(jnp.max(scores, axis=1, keepdims=True))
    exponent = jnp.where(visible, jnp.exp(scores - highest), 0.0)
    weights = exponent.astype(jnp.bfloat16)
    numerator = jnp.dot(weights, values, preferred_element_type=jnp.float32)
    return numerator / lax.optimization_barrier(jnp.sum(exponent, axis=1, keepdims=True))

def reference(queries, cache_keys, cache_values, span_keys, span_values, pool_keys, pool_values, gate_logits, chosen_blocks, valid_counts):
    keys_all = jnp.concatenate([cache_keys, span_keys], axis=0)
    values_all = jnp.concatenate([cache_values, span_values], axis=0)
    comp_keys = pool_blocks(keys_all, jnp.zeros((STRIDE, DK), jnp.bfloat16), pool_keys, STRIDE)
    comp_values = pool_blocks(values_all, jnp.zeros((STRIDE, DV), jnp.bfloat16), pool_values, STRIDE)
    block_ends = jnp.arange(NCB, dtype=jnp.int32) * STRIDE + CLEN
    score_scale = 1.0 / math.sqrt(DK)
    query_tiles = queries.reshape(TILES, BLOCK * HEADS, DK)
    gate_tiles = jax.nn.sigmoid(gate_logits.astype(jnp.float32)).reshape(TILES, BLOCK, 3, HEADS)
    key_blocks = keys_all.reshape(-1, BLOCK, DK)
    value_blocks = values_all.reshape(-1, BLOCK, DV)
    offsets = jnp.arange(BLOCK, dtype=jnp.int32)
    near_offsets = jnp.arange(WINDOW + BLOCK, dtype=jnp.int32)

    def one_tile(tile_number):
        query_rows = query_tiles[tile_number]
        first_pos = (CACHE + tile_number * BLOCK).astype(jnp.int32)
        row_pos = first_pos + jnp.arange(BLOCK * HEADS, dtype=jnp.int32) // HEADS
        comp_out = attend(query_rows, comp_keys, comp_values, block_ends[None, :] <= row_pos[:, None] + 1, score_scale)
        chosen = chosen_blocks[tile_number]
        picked_keys = key_blocks[chosen].reshape(-1, DK)
        picked_values = value_blocks[chosen].reshape(-1, DV)
        key_pos = (chosen[:, None] * BLOCK + offsets[None, :]).reshape(-1)
        usable = jnp.repeat(jnp.arange(PICKS, dtype=jnp.int32) < valid_counts[tile_number], BLOCK)
        sel_out = attend(query_rows, picked_keys, picked_values, usable[None, :] & (key_pos[None, :] <= row_pos[:, None]), score_scale)
        begin = (first_pos - WINDOW).astype(jnp.int32)
        near_keys = lax.dynamic_slice_in_dim(keys_all, begin, WINDOW + BLOCK, 0)
        near_values = lax.dynamic_slice_in_dim(values_all, begin, WINDOW + BLOCK, 0)
        near_pos = begin + near_offsets
        near_visible = (near_pos[None, :] <= row_pos[:, None]) & (near_pos[None, :] > row_pos[:, None] - WINDOW)
        win_out = attend(query_rows, near_keys, near_values, near_visible, score_scale)
        gates = gate_tiles[tile_number]
        mixed = gates[:, 0, :, None] * comp_out.reshape(BLOCK, HEADS, DV) + gates[:, 1, :, None] * sel_out.reshape(BLOCK, HEADS, DV) + gates[:, 2, :, None] * win_out.reshape(BLOCK, HEADS, DV)
        return mixed.reshape(BLOCK, HEADS * DV).astype(jnp.bfloat16)
    result = lax.map(one_tile, jnp.arange(TILES, dtype=jnp.int32))
    return result.reshape(TILES * BLOCK, HEADS * DV)
```

```python
import functools
import math

import jax
import jax.numpy as jnp
import numpy as np
from jax import lax
from jax.experimental import pallas as pl
from jax.experimental.pallas import tpu as pltpu
from jax.sharding import PartitionSpec as P

HEADS = 16
CLEN = 32
STRIDE = 16
BLOCK = 64
HALF = BLOCK // 2
WINDOW = 256
NEG_FILL = -1e30
LANES = 128
GROUP = 4
MESH = pl.DeviceIdType.MESH
F32 = jnp.float32
BF16 = jnp.bfloat16


def pool_rows(rows, extra, weights):
    count, width = rows.shape[0] // STRIDE, rows.shape[1]
    grouped = rows.astype(F32).reshape(count, STRIDE, width)
    leading = jnp.sum(grouped * weights[None, :STRIDE, :], axis=1)
    trailing = jnp.sum(grouped * weights[None, STRIDE:, :], axis=1)
    after = jnp.sum(extra.astype(F32) * weights[STRIDE:, :], axis=0, keepdims=True)
    trailing = jnp.concatenate([trailing[1:], after], axis=0)
    return (leading + trailing).astype(BF16)


def kernel(
    n,
    m,
    queries,
    cache_keys,
    cache_values,
    span_keys,
    span_values,
    pool_keys,
    pool_values,
    gate_logits,
    comp_ends,
    chosen,
    valid,
    out,
    q_in,
    ck,
    cv,
    rk,
    rv,
    packed,
    comp,
    comp_k,
    comp_v,
    heads_k,
    heads_v,
    qa,
    qb,
    sel_k,
    sel_v,
    gates,
    acc,
    bias_comp,
    bias_sel,
    bias_win,
    local_sem,
    head_send,
    head_recv,
    tail_send,
    tail_recv,
    z_send,
    z_recv,
    p_send,
    p_recv,
    s_send,
    s_recv,
    cz_send,
    cz_recv,
    cs_send,
    cs_recv,
):
    c, p, r = lax.axis_index("ctx"), lax.axis_index("pb"), lax.axis_index("row")
    place = p * 2 + r
    cache_len, dk = ck.shape
    span_len = span_keys.shape[0]
    tokens = q_in.shape[0]
    blocks = cache_len // BLOCK
    piece = blocks // (2 * m)
    cache_half, span_half = cache_len // 2, span_len // 2
    comp_cache = cache_half // STRIDE
    picks = chosen.shape[1]
    scale = 1.0 / math.sqrt(dk)
    before, after = lax.rem(c + n - 1, n), lax.rem(c + 1, n)
    tail_parts = WINDOW // BLOCK

    def remote(src, dst, send, recv, ctx=None, pb=None, row=None):
        target = {
            "ctx": c if ctx is None else ctx,
            "pb": p if pb is None else pb,
            "row": r if row is None else row,
        }
        return pltpu.make_async_remote_copy(
            src_ref=src, dst_ref=dst, send_sem=send, recv_sem=recv,
            device_id=target, device_id_type=MESH,
        )

    own_copies = [
        pltpu.make_async_copy(cache_keys, ck, local_sem.at[0]),
        pltpu.make_async_copy(cache_values, cv, local_sem.at[1]),
        pltpu.make_async_copy(span_keys, rk.at[pl.ds(WINDOW, span_len)], local_sem.at[2]),
        pltpu.make_async_copy(span_values, rv.at[pl.ds(WINDOW, span_len)], local_sem.at[3]),
        pltpu.make_async_copy(queries, q_in, local_sem.at[4]),
    ]
    for copy in own_copies:
        copy.start()

    barrier = pltpu.get_barrier_semaphore()
    for k in range(1, n):
        pl.semaphore_signal(
            barrier, inc=1, device_id={"ctx": lax.rem(c + k, n), "pb": p, "row": r},
            device_id_type=MESH,
        )
    for j in range(1, m):
        pl.semaphore_signal(
            barrier, inc=1, device_id={"ctx": c, "pb": lax.rem(p + j, m), "row": r},
            device_id_type=MESH,
        )
    pl.semaphore_signal(
        barrier, inc=1, device_id={"ctx": c, "pb": p, "row": 1 - r}, device_id_type=MESH
    )

    own_copies[0].wait()
    own_copies[1].wait()
    for b in range(blocks):
        low, mid, high = b * BLOCK, b * BLOCK + HALF, (b + 1) * BLOCK
        spot = c * blocks + b
        packed[spot, 0:BLOCK, :] = ck[low:high, :LANES]
        packed[spot, BLOCK : 2 * BLOCK, :] = cv[low:high, :]
        packed[spot, 2 * BLOCK : 2 * BLOCK + HALF, :] = jnp.concatenate(
            [ck[low:mid, LANES:], ck[mid:high, LANES:]], axis=1
        )
    pl.semaphore_wait(barrier, n + m - 1)

    def head_copies(keys, values):
        return [
            remote(keys.at[pl.ds(0, STRIDE)], heads_k.at[0], head_send.at[0], head_recv.at[0], ctx=before),
            remote(values.at[pl.ds(0, STRIDE)], heads_v.at[0], head_send.at[1], head_recv.at[1], ctx=before),
            remote(span_keys.at[pl.ds(0, STRIDE)], heads_k.at[1], head_send.at[2], head_recv.at[2], ctx=before),
            remote(span_values.at[pl.ds(0, STRIDE)], heads_v.at[1], head_send.at[3], head_recv.at[3], ctx=before),
        ]

    @pl.when((r == 1) & (c == 0))
    def _():
        for copy in head_copies(span_keys, span_values):
            copy.start()

    @pl.when((r == 1) & (c != 0))
    def _():
        for copy in head_copies(cache_keys, cache_values):
            copy.start()

    def z_copy(k, owner, target):
        spot = packed.at[pl.ds(owner * blocks + place * piece, piece)]
        return remote(spot, spot, z_send.at[k - 1], z_recv.at[k - 1], ctx=target)

    for k in range(1, n):
        z_copy(k, c, lax.rem(c + n - k, n)).start()

    own_copies[2].wait()
    own_copies[3].wait()

    @pl.when(r == 0)
    def _():
        heads_k[0] = ck[cache_half : cache_half + STRIDE, :]
        heads_v[0] = cv[cache_half : cache_half + STRIDE, :]
        heads_k[1] = rk[WINDOW + span_half : WINDOW + span_half + STRIDE, :]
        heads_v[1] = rv[WINDOW + span_half : WINDOW + span_half + STRIDE, :]

    @pl.when(r == 1)
    def _():
        for copy in head_copies(cache_keys, cache_values):
            copy.wait()

    cache_low = pl.multiple_of(r * cache_half, cache_half)
    span_low = pl.multiple_of(WINDOW + r * span_half, 64)
    weights_k, weights_v = pool_keys[...], pool_values[...]
    comp[c, r, 1] = jnp.zeros(comp.shape[3:], BF16)
    pooled = pool_rows(ck[pl.ds(cache_low, cache_half), :], heads_k[0], weights_k)
    comp[c, r, 0, 0:comp_cache, :] = pooled[:, :LANES]
    comp[c, r, 1, 0:comp_cache, 0 : dk - LANES] = pooled[:, LANES:]
    pooled = pool_rows(rk[pl.ds(span_low, span_half), :], heads_k[1], weights_k)
    comp[c, r, 0, comp_cache:, :] = pooled[:, :LANES]
    comp[c, r, 1, comp_cache:, 0 : dk - LANES] = pooled[:, LANES:]
    comp[c, r, 2, 0:comp_cache, :] = pool_rows(
        cv[pl.ds(cache_low, cache_half), :], heads_v[0], weights_v
    )
    comp[c, r, 2, comp_cache:, :] = pool_rows(
        rv[pl.ds(span_low, span_half), :], heads_v[1], weights_v
    )

    def comp_z(k, owner, target):
        spot = comp.at[owner, r]
        return remote(spot, spot, cz_send.at[k - 1], cz_recv.at[k - 1], ctx=target)

    def comp_s(k, owner, row):
        spot = comp.at[owner, row]
        return remote(spot, spot, cs_send.at[k], cs_recv.at[k], row=1 - r)

    for k in range(1, n):
        comp_z(k, c, lax.rem(c + n - k, n)).start()
    comp_s(0, c, r).start()

    def tail_copies(keys, values, part):
        rows = keys.shape[0]
        source = pl.ds(rows - WINDOW + part * BLOCK, BLOCK)
        dest = pl.ds(part * BLOCK, BLOCK)
        return [
            remote(keys.at[source], rk.at[dest], tail_send.at[part, 0], tail_recv.at[part, 0], ctx=after),
            remote(values.at[source], rv.at[dest], tail_send.at[part, 1], tail_recv.at[part, 1], ctx=after),
        ]

    for part in range(tail_parts):

        @pl.when((place * tokens <= part * BLOCK) & (c == n - 1))
        def _():
            for copy in tail_copies(cache_keys, cache_values, part):
                copy.start()

        @pl.when((place * tokens <= part * BLOCK) & (c != n - 1))
        def _():
            for copy in tail_copies(span_keys, span_values, part):
                copy.start()

    def p_copy(k, j, from_pb, target):
        owner = lax.rem(c + k, n)
        spot = packed.at[pl.ds(owner * blocks + (from_pb * 2 + r) * piece, piece)]
        at = (k - 1) * (m - 1) + j - 1
        return remote(spot, spot, p_send.at[at], p_recv.at[at], pb=target)

    def s_copy(k, j, row):
        owner = lax.rem(c + k, n)
        from_pb = lax.rem(p + m - j, m)
        spot = packed.at[pl.ds(owner * blocks + (from_pb * 2 + row) * piece, piece)]
        at = (k - 1) * m + j
        return remote(spot, spot, s_send.at[at], s_recv.at[at], row=1 - r)

    def forward(k):
        z_copy(k, lax.rem(c + k, n), lax.rem(c + k, n)).wait_recv()
        for j in range(1, m):
            p_copy(k, j, p, lax.rem(p + j, m)).start()
        s_copy(k, 0, r).start()

    def share(k):
        for j in range(1, m):
            p_copy(k, j, lax.rem(p + m - j, m), lax.rem(p + m - j, m)).wait_recv()
            s_copy(k, j, r).start()

    own_copies[4].wait()
    blank = jnp.zeros((tokens, 2 * LANES - dk), BF16)
    for h in range(HEADS):
        low = h * dk
        first, last = q_in[:, low : low + LANES], q_in[:, low + LANES : low + dk]
        rows = pl.ds(h * tokens, tokens)
        qa[rows, 0:LANES] = first
        qb[rows, 0:LANES] = first
        qa[rows, LANES:] = jnp.concatenate([last, blank], axis=1)
        qb[rows, LANES:] = jnp.concatenate([blank, last], axis=1)

    forward(1)

    sigmoid = jax.nn.sigmoid(gate_logits[...].astype(F32))
    for g in range(3):
        for h in range(HEADS):
            column = g * HEADS + h
            gates[g, h * tokens : (h + 1) * tokens, :] = jnp.broadcast_to(
                sigmoid[:, column : column + 1], (tokens, LANES)
            )

    first_pos = n * cache_len + c * span_len + place * tokens
    def token_lane(width):
        return (
            lax.broadcasted_iota(jnp.int32, (tokens, width), 0),
            lax.broadcasted_iota(jnp.int32, (tokens, width), 1),
        )

    token, lane = token_lane(bias_win.shape[1])
    bias_win[...] = jnp.where((lane <= token + WINDOW) & (lane > token), 0.0, NEG_FILL)
    token, lane = token_lane(bias_comp.shape[1])
    bias_comp[...] = jnp.where(comp_ends[...] <= token + (first_pos + 1), 0.0, NEG_FILL)
    token, lane = token_lane(bias_sel.shape[1])
    in_half = picks * HALF
    second = (lane >= in_half).astype(jnp.int32)
    slot = (lane - second * in_half) >> int(math.log2(HALF))
    offset = (lane & (HALF - 1)) + second * HALF
    seen = (slot < valid[0]) & ((slot > 0) | (offset <= token))
    bias_sel[...] = jnp.where(seen, 0.0, NEG_FILL)

    group_rows = GROUP * tokens

    def softmax_out(scores, bias, values):
        width = scores.shape[1]
        scores = (scores * scale).reshape(GROUP, tokens, width) + bias[None]
        scores = scores.reshape(group_rows, width)
        highest = jnp.max(scores, axis=1, keepdims=True)
        exponent = jnp.exp(scores - highest)
        total = jnp.sum(exponent, axis=1, keepdims=True)
        numerator = jnp.dot(exponent.astype(BF16), values, preferred_element_type=F32)
        return numerator / total

    def dot_t(a, b):
        return lax.dot_general(a, b, (((1,), (1,)), ((), ())), preferred_element_type=F32)

    for k in range(2, min(3, n)):
        forward(k)

    for part in range(tail_parts):

        @pl.when(place * tokens <= part * BLOCK)
        def _():
            for copy in tail_copies(span_keys, span_values, part):
                copy.wait()

    near = pl.ds(pl.multiple_of(place * tokens, tokens), WINDOW + tokens)

    @pl.loop(0, HEADS // GROUP)
    def _(g):
        rows = pl.ds(pl.multiple_of(g * group_rows, group_rows), group_rows)
        scores = dot_t(qa[rows, 0:dk], rk[near, :])
        acc[rows, :] = gates[2, rows, :] * softmax_out(scores, bias_win[...], rv[near, :])

    for k in range(3, n):
        forward(k)

    comp_s(0, c, 1 - r).wait_recv()
    for k in range(1, n):
        owner = lax.rem(c + k, n)
        comp_z(k, owner, owner).wait_recv()
        comp_s(k, owner, r).start()
    share(1)
    for k in range(1, n):
        comp_s(k, lax.rem(c + k, n), 1 - r).wait_recv()
    part_rows = comp.shape[3]
    for owner in range(n):
        for row in range(2):
            low = (owner * 2 + row) * part_rows
            comp_k[low : low + part_rows, 0:LANES] = comp[owner, row, 0]
            comp_k[low : low + part_rows, LANES:] = comp[owner, row, 1]
            comp_v[low : low + part_rows, :] = comp[owner, row, 2]

    @pl.loop(0, HEADS // GROUP)
    def _(g):
        rows = pl.ds(pl.multiple_of(g * group_rows, group_rows), group_rows)
        scores = dot_t(qa[rows, :], comp_k[...])
        acc[rows, :] += gates[0, rows, :] * softmax_out(scores, bias_comp[...], comp_v[...])

    for k in range(2, n):
        share(k)
    for k in range(1, n):
        for j in range(m):
            s_copy(k, j, 1 - r).wait_recv()

    own = pl.multiple_of(WINDOW + place * tokens, tokens)
    own_k, own_v = rk[pl.ds(own, BLOCK), :], rv[pl.ds(own, BLOCK), :]
    own_tail = jnp.concatenate([own_k[:HALF, LANES:], own_k[HALF:, LANES:]], axis=1)
    for s in range(picks):
        if s == 0:
            key_rows, value_rows, tail = own_k[:, :LANES], own_v, own_tail
        else:
            number = chosen[0, s]
            key_rows = packed[number, 0:BLOCK, :]
            value_rows = packed[number, BLOCK : 2 * BLOCK, :]
            tail = packed[number, 2 * BLOCK : 2 * BLOCK + HALF, :]
        for part in range(2):
            low = part * in_half + s * HALF
            sel_k[low : low + HALF, 0:LANES] = key_rows[part * HALF : (part + 1) * HALF]
            sel_k[low : low + HALF, LANES:] = tail
            sel_v[low : low + HALF, :] = value_rows[part * HALF : (part + 1) * HALF]

    @pl.loop(0, HEADS // GROUP)
    def _(g):
        rows = pl.ds(pl.multiple_of(g * group_rows, group_rows), group_rows)
        scores = jnp.concatenate(
            [dot_t(qa[rows, :], sel_k[0:in_half, :]), dot_t(qb[rows, :], sel_k[in_half:, :])], axis=1
        )
        mixed = acc[rows, :] + gates[1, rows, :] * softmax_out(scores, bias_sel[...], sel_v[...])
        for i in range(GROUP):
            column = pl.multiple_of((g * GROUP + i) * LANES, LANES)
            out[:, pl.ds(column, LANES)] = mixed[i * tokens : (i + 1) * tokens].astype(BF16)

    for k in range(1, n):
        z_copy(k, c, lax.rem(c + n - k, n)).wait_send()
        comp_z(k, c, lax.rem(c + n - k, n)).wait_send()
        for j in range(1, m):
            p_copy(k, j, p, lax.rem(p + j, m)).wait_send()
        for j in range(m):
            s_copy(k, j, r).wait_send()
    for k in range(n):
        comp_s(k, lax.rem(c + k, n), r).wait_send()


def local(
    queries,
    cache_keys,
    cache_values,
    span_keys,
    span_values,
    pool_keys,
    pool_values,
    gate_logits,
    chosen_blocks,
    valid_counts,
):
    n, m = lax.axis_size("ctx"), lax.axis_size("pb")
    tokens = queries.shape[0]
    cache_len, dk = cache_keys.shape
    dv = cache_values.shape[1]
    span_len = span_keys.shape[0]
    rows = tokens * HEADS
    picks = chosen_blocks.shape[1]
    comp_cache, comp_span = cache_len // 2 // STRIDE, span_len // 2 // STRIDE
    part_rows = comp_cache + comp_span
    shares = np.arange(n * 2)[:, None]
    ids = np.concatenate(
        [
            shares * comp_cache + np.arange(comp_cache)[None],
            2 * n * comp_cache + shares * comp_span + np.arange(comp_span)[None],
        ],
        axis=1,
    ).reshape(1, -1)
    comp_ends = jnp.asarray(ids * STRIDE + CLEN, dtype=jnp.int32)
    blocks = cache_len // BLOCK
    sem = pltpu.SemaphoreType.DMA
    anywhere = pl.BlockSpec(memory_space=pl.ANY)
    vmem = pl.BlockSpec(memory_space=pltpu.VMEM)
    smem = pl.BlockSpec(memory_space=pltpu.SMEM)
    keys = n * 2 * part_rows + picks * BLOCK + WINDOW + tokens
    return pl.pallas_call(
        functools.partial(kernel, n, m),
        out_shape=jax.ShapeDtypeStruct((tokens, HEADS * dv), BF16),
        in_specs=[anywhere] * 5 + [vmem] * 4 + [smem] * 2,
        out_specs=vmem,
        scratch_shapes=[
            pltpu.VMEM((tokens, HEADS * dk), BF16),
            pltpu.VMEM((cache_len, dk), BF16),
            pltpu.VMEM((cache_len, dv), BF16),
            pltpu.VMEM((WINDOW + span_len, dk), BF16),
            pltpu.VMEM((WINDOW + span_len, dv), BF16),
            pltpu.VMEM((n * blocks, 2 * BLOCK + HALF, LANES), BF16),
            pltpu.VMEM((n, 2, 3, part_rows, LANES), BF16),
            pltpu.VMEM((n * 2 * part_rows, 2 * LANES), BF16),
            pltpu.VMEM((n * 2 * part_rows, dv), BF16),
            pltpu.VMEM((2, STRIDE, dk), BF16),
            pltpu.VMEM((2, STRIDE, dv), BF16),
            pltpu.VMEM((rows, 2 * LANES), BF16),
            pltpu.VMEM((rows, 2 * LANES), BF16),
            pltpu.VMEM((picks * BLOCK, 2 * LANES), BF16),
            pltpu.VMEM((picks * BLOCK, dv), BF16),
            pltpu.VMEM((3, rows, LANES), F32),
            pltpu.VMEM((rows, dv), F32),
            pltpu.VMEM((tokens, n * 2 * part_rows), F32),
            pltpu.VMEM((tokens, picks * BLOCK), F32),
            pltpu.VMEM((tokens, WINDOW + tokens), F32),
            sem((5,)),
            sem((4,)),
            sem((4,)),
            sem((WINDOW // BLOCK, 2)),
            sem((WINDOW // BLOCK, 2)),
            sem((n - 1,)),
            sem((n - 1,)),
            sem(((n - 1) * (m - 1),)),
            sem(((n - 1) * (m - 1),)),
            sem(((n - 1) * m,)),
            sem(((n - 1) * m,)),
            sem((n - 1,)),
            sem((n - 1,)),
            sem((n,)),
            sem((n,)),
        ],
        compiler_params=pltpu.CompilerParams(
            collective_id=0, has_side_effects=True, vmem_limit_bytes=48 * 1024 * 1024
        ),
        cost_estimate=pl.CostEstimate(
            flops=2 * rows * keys * (dk + dv),
            bytes_accessed=4 * 1024 * 1024,
            transcendentals=rows * keys,
        ),
    )(
        queries,
        cache_keys,
        cache_values,
        span_keys,
        span_values,
        pool_keys,
        pool_values,
        gate_logits,
        comp_ends,
        chosen_blocks,
        valid_counts,
    )


def solution(mesh):
    spread = P(("parts", "ctx", "pb", "row"), None)
    shard = P(("parts", "ctx"), None)
    return jax.shard_map(
        local,
        mesh=mesh,
        in_specs=(
            spread,
            shard,
            shard,
            shard,
            shard,
            P(),
            P(),
            spread,
            spread,
            P(("parts", "ctx", "pb", "row")),
        ),
        out_specs=spread,
        check_vma=False,
    )
```

```python
import functools
import math

import jax
import jax.numpy as jnp
import numpy as np
from jax import lax
from jax.experimental import pallas as pl
from jax.experimental.pallas import tpu as pltpu
from jax.sharding import PartitionSpec as P

HEADS = 16
CLEN = 32
STRIDE = 16
BLOCK = 64
WINDOW = 256
NEG_FILL = -1e30
LANES = 128
GROUP = 16
MESH = pl.DeviceIdType.MESH
F32 = jnp.float32
BF16 = jnp.bfloat16


def pool_rows(rows, extra, weights):
    count, width = rows.shape[0] // STRIDE, rows.shape[1]
    grouped = rows.astype(F32).reshape(count, STRIDE, width)
    leading = jnp.sum(grouped * weights[None, :STRIDE, :], axis=1)
    trailing = jnp.sum(grouped * weights[None, STRIDE:, :], axis=1)
    after = jnp.sum(extra.astype(F32) * weights[STRIDE:, :], axis=0, keepdims=True)
    trailing = jnp.concatenate([trailing[1:], after], axis=0)
    return (leading + trailing).astype(BF16)


def kernel(
    n,
    m,
    queries,
    cache_keys,
    cache_values,
    span_keys,
    span_values,
    pool_keys,
    pool_values,
    gate_logits,
    comp_ends,
    chosen,
    valid,
    out,
    q_in,
    packed,
    near,
    comp,
    comp_k,
    comp_v,
    lead_k,
    lead_v,
    heads_k,
    heads_v,
    qa,
    sel_k,
    sel_v,
    gates,
    acc,
    bias_comp,
    bias_sel,
    bias_win,
    q_sem,
    cache_sem,
    span_sem,
    head_send,
    head_recv,
    tail_send,
    tail_recv,
    pair_send,
    pair_recv,
    z_send,
    z_recv,
    p_send,
    p_recv,
    s_send,
    s_recv,
    cz_send,
    cz_recv,
    cs_send,
    cs_recv,
):
    c, p, r = lax.axis_index("ctx"), lax.axis_index("pb"), lax.axis_index("row")
    place = p * 2 + r
    dk, cache_len = cache_keys.shape
    span_len = span_keys.shape[1]
    tokens = q_in.shape[0]
    tiles, span_tiles, tail_tiles = cache_len // LANES, span_len // LANES, WINDOW // LANES
    tile_rows = packed.shape[1]
    comp_cache = cache_len // 2 // STRIDE
    picks = chosen.shape[1]
    scale = 1.0 / math.sqrt(dk)
    before, after = lax.rem(c + n - 1, n), lax.rem(c + 1, n)

    def remote(src, dst, send, recv, ctx=None, pb=None, row=None):
        target = {
            "ctx": c if ctx is None else ctx,
            "pb": p if pb is None else pb,
            "row": r if row is None else row,
        }
        return pltpu.make_async_remote_copy(
            src_ref=src, dst_ref=dst, send_sem=send, recv_sem=recv,
            device_id=target, device_id_type=MESH,
        )

    cache_copies, span_copies = [], []
    for i in range(tiles):
        lanes, spot = pl.ds(i * LANES, LANES), packed.at[c * tiles + i]
        cache_copies += [
            pltpu.make_async_copy(cache_keys.at[:, lanes], spot.at[pl.ds(0, dk)], cache_sem.at[i, 0]),
            pltpu.make_async_copy(cache_values.at[lanes], spot.at[pl.ds(dk, LANES)], cache_sem.at[i, 1]),
        ]
    for i in range(span_tiles):
        lanes, spot = pl.ds(i * LANES, LANES), near.at[tail_tiles + i]
        span_copies += [
            pltpu.make_async_copy(span_keys.at[:, lanes], spot.at[pl.ds(0, dk)], span_sem.at[i, 0]),
            pltpu.make_async_copy(span_values.at[lanes], spot.at[pl.ds(dk, LANES)], span_sem.at[i, 1]),
        ]
    q_copy = pltpu.make_async_copy(queries, q_in, q_sem.at[0])
    for copy in cache_copies + span_copies + [q_copy]:
        copy.start()

    barrier = pltpu.get_barrier_semaphore()
    for k in range(1, n):
        pl.semaphore_signal(
            barrier, inc=1, device_id={"ctx": lax.rem(c + k, n), "pb": p, "row": r},
            device_id_type=MESH,
        )
    for j in range(1, m):
        pl.semaphore_signal(
            barrier, inc=1, device_id={"ctx": c, "pb": lax.rem(p + j, m), "row": r},
            device_id_type=MESH,
        )
    pl.semaphore_signal(
        barrier, inc=1, device_id={"ctx": c, "pb": p, "row": 1 - r}, device_id_type=MESH
    )
    for copy in cache_copies + span_copies:
        copy.wait()

    def own_tile(i):
        return packed[c * tiles + i, 0:dk, :].T, packed[c * tiles + i, dk:, :]

    def span_tile(i):
        return near[tail_tiles + i, 0:dk, :].T, near[tail_tiles + i, dk:, :]

    keys, values = own_tile(0)
    lead_k[0], lead_v[0] = keys[:STRIDE], values[:STRIDE]
    keys, values = span_tile(0)
    lead_k[1], lead_v[1] = keys[:STRIDE], values[:STRIDE]

    def head_copies(first):
        return [
            remote(lead_k.at[first], heads_k.at[0], head_send.at[0], head_recv.at[0], ctx=before),
            remote(lead_v.at[first], heads_v.at[0], head_send.at[1], head_recv.at[1], ctx=before),
            remote(lead_k.at[1], heads_k.at[1], head_send.at[2], head_recv.at[2], ctx=before),
            remote(lead_v.at[1], heads_v.at[1], head_send.at[3], head_recv.at[3], ctx=before),
        ]

    pl.semaphore_wait(barrier, n + m - 1)

    @pl.when((r == 1) & (c == 0))
    def _():
        for copy in head_copies(1):
            copy.start()

    @pl.when((r == 1) & (c != 0))
    def _():
        for copy in head_copies(0):
            copy.start()

    def tail_copy(source, part):
        return remote(source, near.at[part], tail_send.at[part], tail_recv.at[part], ctx=after)

    def pair_copy(part):
        return remote(near.at[part], near.at[part], pair_send.at[part], pair_recv.at[part], row=1 - r)

    for part in range(tail_tiles):

        @pl.when((p <= part) & (r == part % 2) & (c == n - 1))
        def _():
            tail_copy(packed.at[c * tiles + tiles - tail_tiles + part], part).start()

        @pl.when((p <= part) & (r == part % 2) & (c != n - 1))
        def _():
            tail_copy(near.at[span_tiles + part], part).start()

    def piece_of(owner, index):
        if tiles >= 2 * m:
            step = tiles // (2 * m)
            return packed.at[pl.ds(owner * tiles + index * step, step)]
        parts = 2 * m // tiles
        rows = tile_rows // parts
        return packed.at[owner * tiles + index // parts, pl.ds(lax.rem(index, parts) * rows, rows)]

    def z_copy(k, owner, target):
        spot = piece_of(owner, place)
        return remote(spot, spot, z_send.at[k - 1], z_recv.at[k - 1], ctx=target)

    for k in range(1, n):
        z_copy(k, c, lax.rem(c + n - k, n)).start()

    def p_copy(k, j, from_pb, target):
        spot = piece_of(lax.rem(c + k, n), from_pb * 2 + r)
        at = (k - 1) * (m - 1) + j - 1
        return remote(spot, spot, p_send.at[at], p_recv.at[at], pb=target)

    def s_copy(k, j, row):
        spot = piece_of(lax.rem(c + k, n), lax.rem(p + m - j, m) * 2 + row)
        at = (k - 1) * m + j
        return remote(spot, spot, s_send.at[at], s_recv.at[at], row=1 - r)

    def forward(k):
        z_copy(k, lax.rem(c + k, n), lax.rem(c + k, n)).wait_recv()
        for j in range(1, m):
            p_copy(k, j, p, lax.rem(p + j, m)).start()
        s_copy(k, 0, r).start()

    def share(k):
        for j in range(1, m):
            p_copy(k, j, lax.rem(p + m - j, m), lax.rem(p + m - j, m)).wait_recv()
            s_copy(k, j, r).start()

    @pl.when(r == 0)
    def _():
        keys, values = own_tile(tiles // 2)
        heads_k[0], heads_v[0] = keys[:STRIDE], values[:STRIDE]
        keys, values = span_tile(span_tiles // 2)
        heads_k[1], heads_v[1] = keys[:STRIDE], values[:STRIDE]

    weights_k, weights_v = pool_keys[...], pool_values[...]

    def half_of(tile_at, count):
        pairs = [tile_at(r * count + i) for i in range(count)]
        return (
            jnp.concatenate([pair[0] for pair in pairs], axis=0),
            jnp.concatenate([pair[1] for pair in pairs], axis=0),
        )

    cache_half = half_of(own_tile, tiles // 2)
    span_half = half_of(span_tile, span_tiles // 2)

    @pl.when(r == 1)
    def _():
        for copy in head_copies(0):
            copy.wait()

    comp[c, r, 1] = jnp.zeros(comp.shape[3:], BF16)
    for which, (keys, values), rows in (
        (0, cache_half, slice(0, comp_cache)),
        (1, span_half, slice(comp_cache, None)),
    ):
        pooled = pool_rows(keys, heads_k[which], weights_k)
        comp[c, r, 0, rows, :] = pooled[:, :LANES]
        comp[c, r, 1, rows, 0 : dk - LANES] = pooled[:, LANES:]
        comp[c, r, 2, rows, :] = pool_rows(values, heads_v[which], weights_v)

    def comp_z(k, owner, target):
        spot = comp.at[owner, r]
        return remote(spot, spot, cz_send.at[k - 1], cz_recv.at[k - 1], ctx=target)

    def comp_s(k, owner, row):
        spot = comp.at[owner, row]
        return remote(spot, spot, cs_send.at[k], cs_recv.at[k], row=1 - r)

    for k in range(1, n):
        comp_z(k, c, lax.rem(c + n - k, n)).start()
    comp_s(0, c, r).start()

    q_copy.wait()
    qa[:, dk:] = jnp.zeros((qa.shape[0], 2 * LANES - dk), BF16)
    for h in range(HEADS):
        qa[h * tokens : (h + 1) * tokens, 0:dk] = q_in[:, h * dk : (h + 1) * dk]

    for part in range(tail_tiles):

        @pl.when((p <= part) & (r == part % 2))
        def _():
            tail_copy(near.at[span_tiles + part], part).wait()
            pair_copy(part).start()

    forward(1)

    sigmoid = jax.nn.sigmoid(gate_logits[...].astype(F32).T)
    for g in range(3):
        for h in range(HEADS):
            column = g * HEADS + h
            gates[g, h * tokens : (h + 1) * tokens, :] = jnp.broadcast_to(
                sigmoid[:, column : column + 1], (tokens, LANES)
            )

    first_pos = n * cache_len + c * span_len + place * tokens

    def token_lane(width):
        return (
            lax.broadcasted_iota(jnp.int32, (tokens, width), 0),
            lax.broadcasted_iota(jnp.int32, (tokens, width), 1),
        )

    token, lane = token_lane(bias_win.shape[1])
    token = token + r * tokens
    bias_win[...] = jnp.where((lane <= token + WINDOW) & (lane > token), 0.0, NEG_FILL)
    token, lane = token_lane(bias_comp.shape[1])
    bias_comp[...] = jnp.where(comp_ends[...] <= token + (first_pos + 1), 0.0, NEG_FILL)
    token, lane = token_lane(bias_sel.shape[1])
    slot, offset = lane >> int(math.log2(BLOCK)), lane & (BLOCK - 1)
    seen = (slot < valid[0]) & ((slot > 0) | (offset <= token))
    bias_sel[...] = jnp.where(seen, 0.0, NEG_FILL)

    group_rows = GROUP * tokens

    def softmax_out(scores, bias, values):
        width = scores.shape[1]
        scores = (scores * scale).reshape(GROUP, tokens, width) + bias[None]
        scores = scores.reshape(group_rows, width)
        highest = jnp.max(scores, axis=1, keepdims=True)
        exponent = jnp.exp(scores - highest)
        total = jnp.sum(exponent, axis=1, keepdims=True)
        numerator = jnp.dot(exponent.astype(BF16), values, preferred_element_type=F32)
        return numerator / total

    for k in range(2, n):
        forward(k)

    for part in range(tail_tiles):

        @pl.when((p <= part) & (r != part % 2))
        def _():
            pair_copy(part).wait_recv()

    near_tiles = [near[p + i] for i in range(tail_tiles + 1)]
    near_k = jnp.concatenate([tile[:dk] for tile in near_tiles], axis=1)
    near_v = jnp.concatenate([tile[dk:] for tile in near_tiles], axis=0)
    sel_k[:, 0 : near_k.shape[1]] = near_k
    sel_v[0 : near_v.shape[0], :] = near_v

    @pl.loop(0, HEADS // GROUP)
    def _(g):
        rows = pl.ds(pl.multiple_of(g * group_rows, group_rows), group_rows)
        scores = jnp.dot(
            qa[rows, 0:dk], sel_k[:, 0 : near_k.shape[1]], preferred_element_type=F32
        )
        acc[rows, :] = gates[2, rows, :] * softmax_out(
            scores, bias_win[...], sel_v[0 : near_v.shape[0], :]
        )

    share(1)

    comp_s(0, c, 1 - r).wait_recv()
    for k in range(1, n):
        owner = lax.rem(c + k, n)
        comp_z(k, owner, owner).wait_recv()
        comp_s(k, owner, r).start()
    for k in range(1, n):
        comp_s(k, lax.rem(c + k, n), 1 - r).wait_recv()
    part_rows = comp.shape[3]
    for owner in range(n):
        for row in range(2):
            low = (owner * 2 + row) * part_rows
            comp_k[low : low + part_rows, 0:LANES] = comp[owner, row, 0]
            comp_k[low : low + part_rows, LANES:] = comp[owner, row, 1]
            comp_v[low : low + part_rows, :] = comp[owner, row, 2]

    @pl.loop(0, HEADS // GROUP)
    def _(g):
        rows = pl.ds(pl.multiple_of(g * group_rows, group_rows), group_rows)
        scores = lax.dot_general(
            qa[rows, :], comp_k[...], (((1,), (1,)), ((), ())), preferred_element_type=F32
        )
        acc[rows, :] += gates[0, rows, :] * softmax_out(scores, bias_comp[...], comp_v[...])

    for k in range(2, n):
        share(k)
    for k in range(1, n):
        for j in range(m):
            s_copy(k, j, 1 - r).wait_recv()

    own = near[tail_tiles + p]
    for s in range(0, picks, 2):
        halves = []
        for slot_at in (s, s + 1):
            if slot_at == 0:
                tile, odd = own, r
            else:
                number = chosen[0, slot_at]
                tile, odd = packed[number >> 1], number & 1
            high = jnp.broadcast_to(odd.astype(F32), (1, BLOCK)).astype(BF16)
            low = jnp.broadcast_to((1 - odd).astype(F32), (1, BLOCK)).astype(BF16)
            halves.append(tile[:dk, :BLOCK] * low + tile[:dk, BLOCK:] * high)
            high = jnp.concatenate([high, high], axis=1)
            low = jnp.concatenate([low, low], axis=1)
            sel_v[slot_at * BLOCK : (slot_at + 1) * BLOCK, :] = (
                tile[dk : dk + BLOCK] * low + tile[dk + BLOCK :] * high
            )
        sel_k[:, s * BLOCK : (s + 2) * BLOCK] = jnp.concatenate(halves, axis=1)

    @pl.loop(0, HEADS // GROUP)
    def _(g):
        rows = pl.ds(pl.multiple_of(g * group_rows, group_rows), group_rows)
        scores = jnp.dot(qa[rows, 0:dk], sel_k[...], preferred_element_type=F32)
        mixed = acc[rows, :] + gates[1, rows, :] * softmax_out(scores, bias_sel[...], sel_v[...])
        for i in range(GROUP):
            column = pl.multiple_of((g * GROUP + i) * LANES, LANES)
            out[:, pl.ds(column, LANES)] = mixed[i * tokens : (i + 1) * tokens].astype(BF16)

    for part in range(tail_tiles):

        @pl.when((p <= part) & (r == part % 2))
        def _():
            pair_copy(part).wait_send()

    for k in range(1, n):
        z_copy(k, c, lax.rem(c + n - k, n)).wait_send()
        comp_z(k, c, lax.rem(c + n - k, n)).wait_send()
        for j in range(1, m):
            p_copy(k, j, p, lax.rem(p + j, m)).wait_send()
        for j in range(m):
            s_copy(k, j, r).wait_send()
    for k in range(n):
        comp_s(k, lax.rem(c + k, n), r).wait_send()


def local(
    queries,
    cache_keys,
    cache_values,
    span_keys,
    span_values,
    pool_keys,
    pool_values,
    gate_logits,
    chosen_blocks,
    valid_counts,
):
    n, m = lax.axis_size("ctx"), lax.axis_size("pb")
    tokens = queries.shape[0]
    cache_len, dk = cache_keys.shape
    dv = cache_values.shape[1]
    span_len = span_keys.shape[0]
    rows = tokens * HEADS
    picks = chosen_blocks.shape[1]
    comp_cache, comp_span = cache_len // 2 // STRIDE, span_len // 2 // STRIDE
    part_rows = comp_cache + comp_span
    shares = np.arange(n * 2)[:, None]
    ids = np.concatenate(
        [
            shares * comp_cache + np.arange(comp_cache)[None],
            2 * n * comp_cache + shares * comp_span + np.arange(comp_span)[None],
        ],
        axis=1,
    ).reshape(1, -1)
    comp_ends = jnp.asarray(ids * STRIDE + CLEN, dtype=jnp.int32)
    tiles, span_tiles, tail_tiles = cache_len // LANES, span_len // LANES, WINDOW // LANES
    sem = pltpu.SemaphoreType.DMA
    anywhere = pl.BlockSpec(memory_space=pl.ANY)
    vmem = pl.BlockSpec(memory_space=pltpu.VMEM)
    smem = pl.BlockSpec(memory_space=pltpu.SMEM)
    keys = n * 2 * part_rows + picks * BLOCK + WINDOW + tokens
    return pl.pallas_call(
        functools.partial(kernel, n, m),
        out_shape=jax.ShapeDtypeStruct((tokens, HEADS * dv), BF16),
        in_specs=[anywhere] * 5 + [vmem] * 4 + [smem] * 2,
        out_specs=vmem,
        scratch_shapes=[
            pltpu.VMEM((tokens, HEADS * dk), BF16),
            pltpu.VMEM((n * tiles, dk + LANES, LANES), BF16),
            pltpu.VMEM((tail_tiles + span_tiles, dk + LANES, LANES), BF16),
            pltpu.VMEM((n, 2, 3, part_rows, LANES), BF16),
            pltpu.VMEM((n * 2 * part_rows, 2 * LANES), BF16),
            pltpu.VMEM((n * 2 * part_rows, dv), BF16),
            pltpu.VMEM((2, STRIDE, dk), BF16),
            pltpu.VMEM((2, STRIDE, dv), BF16),
            pltpu.VMEM((2, STRIDE, dk), BF16),
            pltpu.VMEM((2, STRIDE, dv), BF16),
            pltpu.VMEM((rows, 2 * LANES), BF16),
            pltpu.VMEM((dk, picks * BLOCK), BF16),
            pltpu.VMEM((picks * BLOCK, dv), BF16),
            pltpu.VMEM((3, rows, LANES), F32),
            pltpu.VMEM((rows, dv), F32),
            pltpu.VMEM((tokens, n * 2 * part_rows), F32),
            pltpu.VMEM((tokens, picks * BLOCK), F32),
            pltpu.VMEM((tokens, (tail_tiles + 1) * LANES), F32),
            sem((1,)),
            sem((tiles, 2)),
            sem((span_tiles, 2)),
            sem((4,)),
            sem((4,)),
            sem((tail_tiles,)),
            sem((tail_tiles,)),
            sem((tail_tiles,)),
            sem((tail_tiles,)),
            sem((n - 1,)),
            sem((n - 1,)),
            sem(((n - 1) * (m - 1),)),
            sem(((n - 1) * (m - 1),)),
            sem(((n - 1) * m,)),
            sem(((n - 1) * m,)),
            sem((n - 1,)),
            sem((n - 1,)),
            sem((n,)),
            sem((n,)),
        ],
        compiler_params=pltpu.CompilerParams(
            collective_id=0, has_side_effects=True, vmem_limit_bytes=60 * 1024 * 1024
        ),
        cost_estimate=pl.CostEstimate(
            flops=2 * rows * keys * (dk + dv),
            bytes_accessed=4 * 1024 * 1024,
            transcendentals=rows * keys,
        ),
    )(
        queries,
        cache_keys.T,
        cache_values,
        span_keys.T,
        span_values,
        pool_keys,
        pool_values,
        gate_logits.T,
        comp_ends,
        chosen_blocks,
        valid_counts,
    )


def solution(mesh):
    spread = P(("parts", "ctx", "pb", "row"), None)
    shard = P(("parts", "ctx"), None)
    return jax.shard_map(
        local,
        mesh=mesh,
        in_specs=(
            spread,
            shard,
            shard,
            shard,
            shard,
            P(),
            P(),
            spread,
            spread,
            P(("parts", "ctx", "pb", "row")),
        ),
        out_specs=spread,
        check_vma=False,
    )
```
